32 devices in a mesh: seq: 4 (over z), tp: 2 (over y), rep: 4 (over x, core).
Axes of the slice: x: 2, y: 2, z: 4, core: 2. Of those that a mesh axis runs over, the one named last changes fastest.
Arguments:
- counts: int32 [4, 4], P('rep'), may hold values from 1 to 160, 256 in all within a row
- prompt_of: int32 [4, 256], P('rep'), may hold values from 0 to 7, as said below
- queries: bfloat16 [4, 640, 8192], P('rep', 'seq', 'tp'), may hold values from -10 to 10
- new_kv: bfloat16 [4, 640, 2, 1024], P('rep', 'seq', None, 'tp'), may hold values from -10 to 10
- prompt_keys: bfloat16 [4, 8, 4096, 1024], P('rep', None, 'seq', 'tp'), may hold values from -6 to 6
- prompt_values: bfloat16 [4, 8, 4096, 1024], P('rep', None, 'seq', 'tp'), may hold values from -6 to 6
- suffix_keys: bfloat16 [4, 256, 64, 1024], P('rep', 'seq', None, 'tp'), may hold values from -9 to 9
- suffix_values: bfloat16 [4, 256, 64, 1024], P('rep', 'seq', None, 'tp'), may hold values from -6 to 6
- gen_len: int32 [4, 256], P('rep', 'seq'), may hold values from 1 to 64, 8192 in all within a row
- out_weight: bfloat16 [8192, 8192], P('tp', ('seq', 'rep')), may hold values from -0.0625 to 0.0625
Outputs:
- projected: bfloat16 [1024, 8192], P('tp', ('seq', 'rep'))
The draws below stay inside these ranges and needn't reach their ends.
Inputs may be any that keep to these rules, and one draw needn't show every extreme that they name: In each group the live slots of seq index s are its first counts[s] slots; together they hold the group's rows in order. `prompt_of`: in each group every prompt is named by exactly 32 rows.
All inputs are finite; a program needn't handle non-finite values. No bound on the sum of `gen_len` on one device may be relied on, other than what follows from the above.
Results may differ from the reference program's by a relative error of at most 0.014.
Values may be sent and summed in bfloat16 or wider, within the bound.
A program may use at most 128 MiB of HBM per device.

```python
import math
import jax
import jax.numpy as jnp
import numpy as np
from jax import lax

D = 8192
HEADS = 64
KV_HEADS = 8
HD = 128
ANSWERS = 32
P_GRP = 8
PROMPT_DEV = 1024
SUF_MAX = 64
ROWS_GRP = 256
CAP = 160
PROMPT_LEN = 4096
N_SEQ = 4
N_REP = 4


def draw_prompt_of(key, part):
    rows = P_GRP * ANSWERS
    keys = jax.random.split(jax.random.fold_in(key, 77), N_REP)
    orders = jax.vmap(lambda one: jax.random.permutation(one, rows))(keys)
    return (orders // ANSWERS).astype(jnp.int32)


def draw_queries(key, part):
    slots = N_SEQ * CAP
    shape = (N_REP, slots, HEADS * HD)
    return jnp.clip(2.5 * jax.random.normal(jax.random.fold_in(key, 1), shape, jnp.float32), -10.0, 10.0).astype(jnp.bfloat16)


def draw_prompt_keys(key, part):
    length = PROMPT_DEV * N_SEQ
    shape = (N_REP, P_GRP, length, KV_HEADS * HD)
    return jnp.clip(jax.random.normal(jax.random.fold_in(key, 5), shape, jnp.float32), -6.0, 6.0).astype(jnp.bfloat16)


def shard_levels(rng, extent, shards, low, high):
    def one(dim, shards_of):
        heights = jax.random.uniform(jax.random.fold_in(jax.random.fold_in(rng, 6), dim), (shards_of,), jnp.float32, low / len(shards), high / len(shards))
        return jnp.repeat(jnp.exp(heights), extent[dim] // shards_of).reshape((-1,) + (1,) * (len(extent) - dim - 1))

    gain = one(*shards[0])
    for cut in shards[1:]:
        gain = gain * one(*cut)
    return gain


def split_up(amount, total, bound, lean):
    weights = [(1 << 20) // math.isqrt(standing ** lean) + 1 for standing in range(2, amount + 1)]
    rest, given = total - bound - (amount - 1), [1] * (amount - 1)
    while rest > 0:
        free = [i for i in range(amount - 1) if given[i] < bound]
        mass, left = sum([weights[i] for i in free]), rest
        for i in free:
            addition = min(bound - given[i], max(1, left * weights[i] // mass), rest)
            given[i] = given[i] + addition
            rest = rest - addition
    return np.array([bound] + given)


def uneven_parts(own_key, number_of, total, reach, lean):
    if number_of == 2:
        one = jax.random.randint(own_key, (), max(1, total - reach), min(reach, total - 1) + 1)
        return jnp.stack([one, total - one])
    tallies = jnp.asarray(split_up(number_of, total, reach, lean), jnp.int32)
    pairs = (number_of - 1) // 2
    donor, taker = tallies[1:1 + 2 * pairs:2], tallies[2:2 + 2 * pairs:2]
    room = jnp.minimum(donor - 1, reach - taker)
    moved = jax.random.randint(jax.random.fold_in(own_key, 1), (pairs,), 0, 1 << 20) % (room + 1)
    tallies = tallies.at[1:1 + 2 * pairs:2].set(donor - moved).at[2:2 + 2 * pairs:2].set(taker + moved)
    return tallies[jax.random.permutation(jax.random.fold_in(own_key, 2), number_of)]


def normal_values(own_key, shape, spread, bound, cuts=(), kind=jnp.bfloat16):
    result = jax.random.normal(own_key, shape, jnp.float32) * spread
    if len(cuts) > 0:
        result = shard_levels(own_key, shape, cuts, -0.22, 0.18) * result
    return jnp.clip(result, min=-bound, max=bound).astype(kind)


def setup_inputs(seed: int = 0) -> dict:
    splits = jax.random.split(jax.random.key(seed), 11)
    counts = jax.vmap(lambda own: uneven_parts(own, N_SEQ, ROWS_GRP, CAP, 2))(jax.random.split(splits[0], N_REP)).reshape((N_REP, N_SEQ)).astype(jnp.int32)
    prompt_of = draw_prompt_of(jax.random.fold_in(splits[10], 71), 0)
    queries = draw_queries(jax.random.fold_in(splits[10], 71), 0)
    new_kv = normal_values(splits[3], (N_REP, N_SEQ * CAP, 2, KV_HEADS * HD), 2.0, 10.0, ((0, 4), (1, 4), (3, 2)))
    prompt_keys = draw_prompt_keys(jax.random.fold_in(splits[10], 71), 0)
    prompt_values = normal_values(splits[5], (N_REP, P_GRP, PROMPT_LEN, KV_HEADS * HD), 1.0, 6.0, ((0, 4), (2, 4), (3, 2)))
    suffix_keys = normal_values(splits[6], (N_REP, ROWS_GRP, SUF_MAX, KV_HEADS * HD), 1.5, 9.0, ((0, 4), (1, 4), (3, 2)))
    suffix_values = normal_values(splits[7], (N_REP, ROWS_GRP, SUF_MAX, KV_HEADS * HD), 1.0, 6.0, ((0, 4), (1, 4), (3, 2)))
    gen_len = jax.vmap(lambda own: uneven_parts(own, ROWS_GRP, ROWS_GRP * SUF_MAX // 2, SUF_MAX, 1))(jax.random.split(splits[8], N_REP)).reshape((N_REP, ROWS_GRP)).astype(jnp.int32)
    out_weight = normal_values(splits[9], (HEADS * HD, D), (HEADS * HD) ** -0.5, 0.0625, ((0, 2), (1, 16)))
    return dict(counts=counts, prompt_of=prompt_of, queries=queries, new_kv=new_kv, prompt_keys=prompt_keys, prompt_values=prompt_values, suffix_keys=suffix_keys, suffix_values=suffix_values, gen_len=gen_len, out_weight=out_weight)


def reference(counts, prompt_of, queries, new_kv, prompt_keys, prompt_values, suffix_keys, suffix_values, gen_len, out_weight):
    scale = HD ** -0.5
    share = HEADS // KV_HEADS
    pieces = []
    for group in range(N_REP):
        tally = counts[group].astype(jnp.int32)
        ends = jnp.cumsum(tally).astype(jnp.int32)
        starts = (ends - tally).astype(jnp.int32)
        row_ids = jnp.arange(ROWS_GRP, dtype=jnp.int32)
        holder = jnp.sum((ends[None, :] <= row_ids[:, None]).astype(jnp.int32), axis=1).astype(jnp.int32)
        slot_ids = (holder * CAP + row_ids - starts[holder]).astype(jnp.int32)
        row_queries = queries[group][slot_ids]
        row_kv = new_kv[group][slot_ids]
        group_keys = prompt_keys[group]
        group_values = prompt_values[group]

        def one_row(items):
            query, fresh, prompt, cache_k, cache_v, length = items
            keys = jnp.concatenate([lax.dynamic_index_in_dim(group_keys, prompt, 0, keepdims=False), cache_k, fresh[0][None, :]], axis=0)
            values = jnp.concatenate([lax.dynamic_index_in_dim(group_values, prompt, 0, keepdims=False), cache_v, fresh[1][None, :]], axis=0)
            query_f = query.astype(jnp.float32).reshape(KV_HEADS, share, HD)
            keys_f = keys.astype(jnp.float32).reshape(-1, KV_HEADS, HD)
            values_f = values.astype(jnp.float32).reshape(-1, KV_HEADS, HD)
            scores = jnp.einsum("kgd,lkd->kgl", query_f, keys_f) * scale
            valid = jnp.concatenate([jnp.ones((PROMPT_LEN,), bool), jnp.arange(SUF_MAX, dtype=jnp.int32) < length, jnp.ones((1,), bool)])
            scores = jnp.where(valid[None, None, :], scores, -jnp.inf)
            peak = jnp.max(scores, axis=-1, keepdims=True)
            weights = jnp.exp(scores - peak)
            total = jnp.sum(weights, axis=-1)
            rounded = lax.optimization_barrier(weights.astype(jnp.bfloat16)).astype(jnp.float32)
            mixed = jnp.einsum("kgl,lkd->kgd", rounded, values_f)
            return (mixed / total[..., None]).reshape(HEADS * HD).astype(jnp.bfloat16)

        attended = lax.map(one_row, (row_queries, row_kv, prompt_of[group].astype(jnp.int32), suffix_keys[group], suffix_values[group], gen_len[group].astype(jnp.int32)))
        pieces.append(attended)
    every_row = jnp.concatenate(pieces, axis=0)
    return jnp.dot(every_row, out_weight, preferred_element_type=jnp.float32).astype(jnp.bfloat16)
```

```python
import functools

import jax
import jax.numpy as jnp
from jax import lax
from jax.experimental import pallas as pl
from jax.experimental.pallas import tpu as pltpu
from jax.sharding import PartitionSpec as P

HD = 128
CHUNK = 512
SUF_ROWS = 16
NEG = -1e30
MESH = pl.DeviceIdType.MESH
VMEM_LIMIT = 48 * 1024 * 1024
F32 = jnp.float32
BF16 = jnp.bfloat16


def signal(**where):
    pl.semaphore_signal(
        pltpu.get_barrier_semaphore(), inc=1, device_id=where, device_id_type=MESH
    )


def greet_line(me, n):
    @pl.when(me > 0)
    def _():
        signal(seq=me - 1)

    @pl.when(me < n - 1)
    def _():
        signal(seq=me + 1)


def await_greetings(me, n, others=0):
    line = jnp.minimum(me, 1) + jnp.minimum(n - 1 - me, 1)
    pl.semaphore_wait(pltpu.get_barrier_semaphore(), line + others)


def remote(src, dst, send, recv, **where):
    return pltpu.make_async_remote_copy(
        src_ref=src, dst_ref=dst, send_sem=send, recv_sem=recv, device_id=where, device_id_type=MESH
    )


def spread_kernel(n, pick_ref, q_ref, out_ref, mine, from_left, from_right, to_right, to_left,
                  send_r, recv_r, send_l, recv_l):
    me = lax.axis_index("seq")
    chunks = mine.shape[0]
    if n > 1:
        greet_line(me, n)
    for c in range(chunks):
        mine[c] = jnp.dot(
            pick_ref[...], q_ref[:, c * CHUNK:(c + 1) * CHUNK], preferred_element_type=F32
        ).astype(BF16)
    if n == 1:
        out_ref[...] = mine[...]
        return
    await_greetings(me, n)

    def right(c):
        return remote(to_right.at[c], from_left.at[c], send_r.at[c], recv_r.at[c], seq=me + 1)

    def left(c):
        return remote(to_left.at[c], from_right.at[c], send_l.at[c], recv_l.at[c], seq=me - 1)

    def step(t, carry):
        c = t - me

        @pl.when((c >= 0) & (c < chunks))
        def _():
            @pl.when(me == 0)
            def _():
                to_right[c] = mine[c]

            @pl.when(me > 0)
            def _():
                right(c).wait_recv()
                to_right[c] = from_left[c] + mine[c]

            @pl.when(me < n - 1)
            def _():
                right(c).start()

        e = t - (n - 1 - me)

        @pl.when((e >= 0) & (e < chunks))
        def _():
            @pl.when(me == n - 1)
            def _():
                to_left[e] = mine[e]

            @pl.when(me < n - 1)
            def _():
                left(e).wait_recv()
                to_left[e] = from_right[e] + mine[e]

            @pl.when(me > 0)
            def _():
                left(e).start()

        return carry

    lax.fori_loop(0, chunks + n - 1, step, 0)

    def finish(c, carry):
        @pl.when(me < n - 1)
        def _():
            out_ref[c] = to_right[c] + from_right[c]
            right(c).wait_send()

        @pl.when(me == n - 1)
        def _():
            out_ref[c] = to_right[c]

        @pl.when(me > 0)
        def _():
            left(c).wait_send()

        return carry

    lax.fori_loop(0, chunks, finish, 0)


def prompt_kernel(share, q_ref, k_ref, v_ref, nk_ref, nv_ref, held_ref, o_ref, lse_ref):
    per = CHUNK // HD
    rows = q_ref.shape[1]
    scale = HD ** (-0.5)
    q = jnp.concatenate(
        [q_ref[g // per, :, (g % per) * HD:(g % per + 1) * HD] for g in range(share)], axis=0
    )
    s = lax.dot_general(
        q, k_ref[0], (((1,), (1,)), ((), ())), preferred_element_type=F32
    ) * scale
    nk = jnp.concatenate([nk_ref[...].astype(F32)] * share, axis=0)
    nv = jnp.concatenate([nv_ref[...].astype(F32)] * share, axis=0)
    held = jnp.concatenate([held_ref[...]] * share, axis=0)
    fresh = jnp.sum(q.astype(F32) * nk, axis=1, keepdims=True) * scale
    fresh = jnp.where(held > 0.5, fresh, NEG)
    m = jnp.maximum(jnp.max(s, axis=1, keepdims=True), fresh)
    w = jnp.exp(s - m)
    wn = jnp.exp(fresh - m)
    total = jnp.sum(w, axis=1, keepdims=True) + wn
    o = jnp.dot(w.astype(BF16), v_ref[0], preferred_element_type=F32)
    o = o + wn.astype(BF16).astype(F32) * nv
    o = (o / total).astype(BF16)
    lse = m + jnp.log(total)
    for g in range(share):
        o_ref[:, g * HD:(g + 1) * HD] = o[g * rows:(g + 1) * rows]
    lse_ref[0] = jnp.concatenate([lse[g * rows:(g + 1) * rows] for g in range(share)], axis=1)


def combine_kernel(n, kv_local, share, o_ref, s_ref, q_ref, k_ref, v_ref, len_ref, out_ref,
                   got_o, got_s, suf_o, suf_s, send_o, recv_o, send_s, recv_s):
    me = lax.axis_index("seq")
    rows = q_ref.shape[0]
    span = k_ref.shape[1]
    heads = kv_local * share
    scale = HD ** (-0.5)
    copies = []
    if n > 1:
        for off in range(1, n):
            signal(seq=(me + off) % n)
        pl.semaphore_wait(pltpu.get_barrier_semaphore(), n - 1)
    for off in range(1, n):
        peer = (me + off) % n
        i = off - 1
        copies.append(remote(s_ref.at[peer], got_s.at[i], send_s.at[i], recv_s.at[i], seq=peer))
        copies.append(remote(o_ref.at[peer], got_o.at[i], send_o.at[i], recv_o.at[i], seq=peer))
    for copy in copies:
        copy.start()

    tall, wide = share * SUF_ROWS, SUF_ROWS * span
    at = lax.broadcasted_iota(jnp.int32, (tall, wide), 1)
    own_row = lax.broadcasted_iota(jnp.int32, (tall, wide), 0) % SUF_ROWS
    offset = at - own_row * span

    def suffix(b, carry):
        block = pl.ds(pl.multiple_of(b * SUF_ROWS, SUF_ROWS), SUF_ROWS)
        lens = jnp.concatenate([len_ref[block, :]] * share, axis=0)
        live = (offset >= 0) & (offset < lens)
        found = []
        for h in range(kv_local):
            q = jnp.concatenate(
                [q_ref[block, (h * share + g) * HD:(h * share + g + 1) * HD] for g in range(share)],
                axis=0,
            )
            k = k_ref[block, :, h * HD:(h + 1) * HD].reshape(wide, HD)
            v = v_ref[block, :, h * HD:(h + 1) * HD].reshape(wide, HD)
            s = lax.dot_general(
                q, k, (((1,), (1,)), ((), ())), preferred_element_type=F32
            ) * scale
            s = jnp.where(live, s, NEG)
            m = jnp.max(s, axis=1, keepdims=True)
            w = jnp.exp(s - m)
            total = jnp.sum(w, axis=1, keepdims=True)
            o = jnp.dot(w.astype(BF16), v, preferred_element_type=F32) / total
            lse = m + jnp.log(total)
            for g in range(share):
                part = slice(g * SUF_ROWS, (g + 1) * SUF_ROWS)
                suf_o[block, (h * share + g) * HD:(h * share + g + 1) * HD] = o[part]
                found.append(lse[part])
        if heads < HD:
            found.append(jnp.zeros((SUF_ROWS, HD - heads), F32))
        suf_s[block, :] = jnp.concatenate(found, axis=1)
        return carry

    lax.fori_loop(0, rows // SUF_ROWS, suffix, 0)
    for copy in copies:
        copy.wait()

    stats = [suf_s[...], s_ref[me]] + [got_s[i] for i in range(n - 1)]
    best = functools.reduce(jnp.maximum, stats)
    weights = [jnp.exp(one - best) for one in stats]
    total = functools.reduce(jnp.add, weights)
    weights = [one / total for one in weights]
    for h in range(heads):
        cols = slice(h * HD, (h + 1) * HD)
        mixed = weights[0][:, h:h + 1] * suf_o[:, cols]
        mixed = mixed + weights[1][:, h:h + 1] * o_ref[me, :, cols].astype(F32)
        for i in range(n - 1):
            mixed = mixed + weights[2 + i][:, h:h + 1] * got_o[i, :, cols].astype(F32)
        out_ref[:, cols] = mixed.astype(BF16)


def project_kernel(n, reps, tps, att_ref, w_ref, out_ref, every, parts, got, own,
                   send_r, recv_r, send_l, recv_l, send_x, recv_x, send_t, recv_t, own_sem):
    me, rep, tp = lax.axis_index("seq"), lax.axis_index("rep"), lax.axis_index("tp")
    distances = []
    d = reps // 2
    while d >= 1:
        distances.append(d)
        d //= 2

    def across(r, d):
        return r + d - 2 * d * ((r // d) % 2)

    if n > 1:
        greet_line(me, n)
    for d in distances:
        signal(rep=across(rep, d))
    for off in range(1, tps):
        signal(tp=(tp + off) % tps)
    local = pltpu.make_async_copy(att_ref, every.at[rep * n + me], own_sem)
    local.start()
    local.wait()
    await_greetings(me, n, len(distances) + tps - 1)

    def right(j):
        place = every.at[rep * n + j]
        return remote(place, place, send_r.at[j], recv_r.at[j], seq=me + 1)

    def left(j):
        place = every.at[rep * n + j]
        return remote(place, place, send_l.at[j], recv_l.at[j], seq=me - 1)

    def over(stage, r, j):
        place = every.at[r * n + j]
        return remote(place, place, send_x.at[stage, r * n + j], recv_x.at[r * n + j],
                      rep=across(rep, distances[stage]))

    def hop(t, carry):
        j = me - t

        @pl.when(j >= 0)
        def _():
            @pl.when(t > 0)
            def _():
                right(j).wait_recv()

            @pl.when(me < n - 1)
            def _():
                right(j).start()

            for stage in range(len(distances)):
                over(stage, rep, j).start()

        e = me + t

        @pl.when(e < n)
        def _():
            @pl.when(t > 0)
            def _():
                left(e).wait_recv()
                for stage in range(len(distances)):
                    over(stage, rep, e).start()

            @pl.when(me > 0)
            def _():
                left(e).start()

        return carry

    lax.fori_loop(0, n, hop, 0)

    held = [rep]
    for stage in range(len(distances)):
        arrived = [across(r, distances[stage]) for r in held]
        for r in arrived:
            def pass_on(j, carry, r=r, stage=stage):
                over(stage, r, j).wait_recv()
                for later in range(stage + 1, len(distances)):
                    over(later, r, j).start()
                return carry

            lax.fori_loop(0, n, pass_on, 0)
        held = held + arrived

    blocks, tall = every.shape[0], every.shape[1]
    share = blocks // tps
    unit = min(share, max(1, 256 // tall))

    def rows_of(peer, put):
        def piece(u, carry):
            x = every[pl.ds(peer * share + u * unit, unit)].reshape(unit * tall, -1)
            y = jnp.dot(x, w_ref[...], preferred_element_type=F32)
            put(pl.ds(pl.multiple_of(u * unit * tall, unit * tall), unit * tall), y)
            return carry

        lax.fori_loop(0, share // unit, piece, 0)

    sums = []
    for off in range(1, tps):
        peer = (tp + off) % tps
        i = off - 1

        def put(where, y, i=i):
            parts[i, where, :] = y.astype(BF16)

        rows_of(peer, put)
        copy = remote(parts.at[i], got.at[i], send_t.at[i], recv_t.at[i], tp=peer)
        copy.start()
        sums.append(copy)

    def put_own(where, y):
        own[where, :] = y

    rows_of(tp, put_own)
    for copy in sums:
        copy.wait()
    result = own[...]
    for i in range(tps - 1):
        result = result + got[i].astype(F32)
    out_ref[...] = result.astype(BF16)

    def drain(j, carry):
        @pl.when((j <= me) & (me < n - 1))
        def _():
            right(j).wait_send()

        @pl.when((j >= me) & (me > 0))
        def _():
            left(j).wait_send()

        return carry

    lax.fori_loop(0, n, drain, 0)
    held = [rep]
    for stage in range(len(distances)):
        for r in held:
            def sent(j, carry, r=r, stage=stage):
                over(stage, r, j).wait_send()
                return carry

            lax.fori_loop(0, n, sent, 0)
        held = held + [across(r, distances[stage]) for r in held]


def params(number):
    return pltpu.CompilerParams(
        collective_id=number, has_side_effects=True, vmem_limit_bytes=VMEM_LIMIT
    )


def vmem():
    return pl.BlockSpec(memory_space=pltpu.VMEM)


def body(
    counts,
    prompt_of,
    queries,
    new_kv,
    prompt_keys,
    prompt_values,
    suffix_keys,
    suffix_values,
    gen_len,
    out_weight,
):
    n = lax.axis_size("seq")
    reps = lax.axis_size("rep")
    tps = lax.axis_size("tp")
    me = lax.axis_index("seq")
    capacity, width = queries.shape[1:]
    kv_width = new_kv.shape[3]
    kv_local = kv_width // HD
    heads = width // HD
    share = heads // kv_local
    per_device = gen_len.shape[1]
    group_rows = per_device * n
    prompts, positions = prompt_keys.shape[1:3]
    block_rows = group_rows // prompts
    chunks = width // CHUNK

    tally = counts[0]
    start = jnp.sum(jnp.where(jnp.arange(n, dtype=jnp.int32) < me, tally, 0))
    count = jnp.sum(jnp.where(jnp.arange(n, dtype=jnp.int32) == me, tally, 0))
    row_ids = jnp.arange(group_rows, dtype=jnp.int32)
    of = prompt_of[0]
    before = (of[None, :] < of[:, None]) | (
        (of[None, :] == of[:, None]) & (row_ids[None, :] < row_ids[:, None])
    )
    rank = jnp.sum(before.astype(jnp.int32), axis=1)
    place = (rank[None, :] == row_ids[:, None]).astype(BF16)
    back = (rank[:, None] == row_ids[None, :]).astype(BF16)
    row_of = jnp.sum(jnp.where(rank[None, :] == row_ids[:, None], row_ids[None, :], 0), axis=1)
    slot = row_of - start
    mine = (slot >= 0) & (slot < count)
    picker = (
        (slot[:, None] == jnp.arange(capacity, dtype=jnp.int32)[None, :]) & mine[:, None]
    ).astype(BF16)
    fresh = jnp.dot(
        picker, new_kv[0].reshape(capacity, 2 * kv_width), preferred_element_type=F32
    ).astype(BF16)
    held = mine.astype(F32)[:, None]

    chunk_shape = (chunks, group_rows, CHUNK)
    sorted_q = pl.pallas_call(
        functools.partial(spread_kernel, n),
        out_shape=jax.ShapeDtypeStruct(chunk_shape, BF16),
        in_specs=[vmem(), vmem()],
        out_specs=vmem(),
        scratch_shapes=[pltpu.VMEM(chunk_shape, BF16)] * 5
        + [pltpu.SemaphoreType.DMA((chunks,))] * 4,
        compiler_params=params(0),
        name="spread_queries",
    )(picker, queries[0])

    per = share * HD // CHUNK
    partial_o, lse = pl.pallas_call(
        functools.partial(prompt_kernel, share),
        grid=(kv_local, prompts),
        out_shape=(
            jax.ShapeDtypeStruct((group_rows, width), BF16),
            jax.ShapeDtypeStruct((kv_local, group_rows, share), F32),
        ),
        in_specs=[
            pl.BlockSpec((per, block_rows, CHUNK), lambda h, p: (h, p, 0)),
            pl.BlockSpec((1, positions, HD), lambda h, p: (p, 0, h)),
            pl.BlockSpec((1, positions, HD), lambda h, p: (p, 0, h)),
            pl.BlockSpec((block_rows, HD), lambda h, p: (p, h)),
            pl.BlockSpec((block_rows, HD), lambda h, p: (p, h + kv_local)),
            pl.BlockSpec((block_rows, 1), lambda h, p: (p, 0)),
        ],
        out_specs=(
            pl.BlockSpec((block_rows, share * HD), lambda h, p: (p, h)),
            pl.BlockSpec((1, block_rows, share), lambda h, p: (h, p, 0)),
        ),
        compiler_params=pltpu.CompilerParams(vmem_limit_bytes=VMEM_LIMIT),
        name="prompt_attention",
    )(sorted_q, prompt_keys[0], prompt_values[0], fresh, fresh, held)

    row_o = jnp.dot(back, partial_o, preferred_element_type=F32).astype(BF16)
    row_s = jnp.take(jnp.swapaxes(lse, 0, 1).reshape(group_rows, heads), rank, axis=0)
    row_s = jnp.pad(row_s, ((0, 0), (0, HD - heads)))
    own_back = lax.dynamic_slice_in_dim(back, me * per_device, per_device, 0)
    own_q = jnp.einsum("rp,cpw->rcw", own_back, sorted_q, preferred_element_type=F32)
    own_q = own_q.astype(BF16).reshape(per_device, width)

    attended = pl.pallas_call(
        functools.partial(combine_kernel, n, kv_local, share),
        out_shape=jax.ShapeDtypeStruct((per_device, width), BF16),
        in_specs=[vmem()] * 6,
        out_specs=vmem(),
        scratch_shapes=[
            pltpu.VMEM((max(1, n - 1), per_device, width), BF16),
            pltpu.VMEM((max(1, n - 1), per_device, HD), F32),
            pltpu.VMEM((per_device, width), F32),
            pltpu.VMEM((per_device, HD), F32),
        ]
        + [pltpu.SemaphoreType.DMA((max(1, n - 1),))] * 4,
        compiler_params=params(1),
        name="exchange_and_suffix",
    )(
        row_o.reshape(n, per_device, width),
        row_s.reshape(n, per_device, HD),
        own_q,
        suffix_keys[0],
        suffix_values[0],
        gen_len[0][:, None],
    )

    columns = out_weight.shape[1]
    out_rows = group_rows * reps // tps
    stages = max(1, reps.bit_length() - 1)
    dma = pltpu.SemaphoreType.DMA
    return pl.pallas_call(
        functools.partial(project_kernel, n, reps, tps),
        out_shape=jax.ShapeDtypeStruct((out_rows, columns), BF16),
        in_specs=[vmem()] * 2,
        out_specs=vmem(),
        scratch_shapes=[
            pltpu.VMEM((reps * n, per_device, width), BF16),
            pltpu.VMEM((max(1, tps - 1), out_rows, columns), BF16),
            pltpu.VMEM((max(1, tps - 1), out_rows, columns), BF16),
            pltpu.VMEM((out_rows, columns), F32),
            dma((n,)), dma((n,)), dma((n,)), dma((n,)),
            dma((stages, reps * n)), dma((reps * n,)),
            dma((max(1, tps - 1),)), dma((max(1, tps - 1),)),
            pltpu.SemaphoreType.DMA,
        ],
        compiler_params=params(2),
        name="gather_and_project",
    )(attended, out_weight)


def solution(mesh):
    in_specs = (
        P("rep", None),
        P("rep", None),
        P("rep", "seq", "tp"),
        P("rep", "seq", None, "tp"),
        P("rep", None, "seq", "tp"),
        P("rep", None, "seq", "tp"),
        P("rep", "seq", None, "tp"),
        P("rep", "seq", None, "tp"),
        P("rep", "seq"),
        P("tp", ("seq", "rep")),
    )
    out_specs = P("tp", ("seq", "rep"))
    return jax.shard_map(body, mesh=mesh, in_specs=in_specs, out_specs=out_specs, check_vma=False)
```

```python
import functools

import jax
import jax.numpy as jnp
from jax import lax
from jax.experimental import pallas as pl
from jax.experimental.pallas import tpu as pltpu
from jax.sharding import PartitionSpec as P

HD = 128
CHUNK = 256
PROMPTS_STEP = 4
LOG2E = 1.4426950408889634
SUF_ROWS = 16
NEG = -1e30
MESH = pl.DeviceIdType.MESH
VMEM_LIMIT = 48 * 1024 * 1024
F32 = jnp.float32
BF16 = jnp.bfloat16


def signal(**where):
    pl.semaphore_signal(
        pltpu.get_barrier_semaphore(), inc=1, device_id=where, device_id_type=MESH
    )


def greet_line(me, n):
    @pl.when(me > 0)
    def _():
        signal(seq=me - 1)

    @pl.when(me < n - 1)
    def _():
        signal(seq=me + 1)


def await_greetings(me, n, others=0):
    line = jnp.minimum(me, 1) + jnp.minimum(n - 1 - me, 1)
    pl.semaphore_wait(pltpu.get_barrier_semaphore(), line + others)


def remote(src, dst, send, recv, **where):
    return pltpu.make_async_remote_copy(
        src_ref=src, dst_ref=dst, send_sem=send, recv_sem=recv, device_id=where, device_id_type=MESH
    )


def spread_kernel(n, pick_ref, q_ref, out_ref, mine, from_left, from_right, to_right, to_left,
                  send_r, recv_r, send_l, recv_l):
    me = lax.axis_index("seq")
    chunks = mine.shape[0]
    if n > 1:
        greet_line(me, n)
    for c in range(chunks):
        mine[c] = jnp.dot(
            pick_ref[...], q_ref[:, c * CHUNK:(c + 1) * CHUNK], preferred_element_type=F32
        ).astype(BF16)
    if n == 1:
        out_ref[...] = mine[...]
        return
    await_greetings(me, n)

    def right(c):
        return remote(to_right.at[c], from_left.at[c], send_r.at[c], recv_r.at[c], seq=me + 1)

    def left(c):
        return remote(to_left.at[c], from_right.at[c], send_l.at[c], recv_l.at[c], seq=me - 1)

    def step(t, carry):
        c = t - me

        @pl.when((c >= 0) & (c < chunks))
        def _():
            @pl.when(me == 0)
            def _():
                to_right[c] = mine[c]

            @pl.when(me > 0)
            def _():
                right(c).wait_recv()
                to_right[c] = from_left[c] + mine[c]

            @pl.when(me < n - 1)
            def _():
                right(c).start()

        e = t - (n - 1 - me)

        @pl.when((e >= 0) & (e < chunks))
        def _():
            @pl.when(me == n - 1)
            def _():
                to_left[e] = mine[e]

            @pl.when(me < n - 1)
            def _():
                left(e).wait_recv()
                to_left[e] = from_right[e] + mine[e]

            @pl.when(me > 0)
            def _():
                left(e).start()

        return carry

    lax.fori_loop(0, chunks + n - 1, step, 0)

    def finish(c, carry):
        @pl.when(me < n - 1)
        def _():
            out_ref[c] = to_right[c] + from_right[c]
            right(c).wait_send()

        @pl.when(me == n - 1)
        def _():
            out_ref[c] = to_right[c]

        @pl.when(me > 0)
        def _():
            left(c).wait_send()

        return carry

    lax.fori_loop(0, chunks, finish, 0)


def prompt_kernel(share, q_ref, k_ref, v_ref, nk_ref, nv_ref, held_ref, o_ref, lse_ref):
    per = CHUNK // HD
    prompts = k_ref.shape[0]
    rows = q_ref.shape[1] // prompts
    factor = HD ** (-0.5) * LOG2E
    every = range(prompts)
    spans = [slice(i * rows, (i + 1) * rows) for i in every]
    q = [
        jnp.concatenate(
            [q_ref[g // per, one, (g % per) * HD:(g % per + 1) * HD] for g in range(share)], axis=0
        )
        for one in spans
    ]
    for i, one in enumerate(spans):
        s = lax.dot_general(q[i], k_ref[i], (((1,), (1,)), ((), ())), preferred_element_type=F32)
        nk = jnp.concatenate([nk_ref[one, :].astype(F32)] * share, axis=0)
        nv = jnp.concatenate([nv_ref[one, :].astype(F32)] * share, axis=0)
        held = jnp.concatenate([held_ref[one, :]] * share, axis=0)
        fresh = jnp.sum(q[i].astype(F32) * nk, axis=1, keepdims=True)
        fresh = jnp.where(held > 0.5, fresh, NEG)
        m = jnp.maximum(jnp.max(s, axis=1, keepdims=True), fresh)
        w = jnp.exp2((s - m) * factor)
        wn = jnp.exp2((fresh - m) * factor)
        total = jnp.sum(w, axis=1, keepdims=True) + wn
        o = jnp.dot(w.astype(BF16), v_ref[i], preferred_element_type=F32)
        o = o + wn.astype(BF16).astype(F32) * nv
        o = (o / total).astype(BF16)
        lse = m * HD ** (-0.5) + jnp.log(total)
        for g in range(share):
            o_ref[one, g * HD:(g + 1) * HD] = o[g * rows:(g + 1) * rows]
        lse_ref[0, one, :] = jnp.concatenate(
            [lse[g * rows:(g + 1) * rows] for g in range(share)], axis=1
        )


def combine_kernel(n, kv_local, share, o_ref, s_ref, q_ref, k_ref, v_ref, len_ref, out_ref,
                   got_o, got_s, suf_o, suf_s, send_o, recv_o, send_s, recv_s):
    me = lax.axis_index("seq")
    rows = q_ref.shape[0]
    span = k_ref.shape[1]
    heads = kv_local * share
    scale = HD ** (-0.5)
    copies = []
    if n > 1:
        for off in range(1, n):
            signal(seq=(me + off) % n)
        pl.semaphore_wait(pltpu.get_barrier_semaphore(), n - 1)
    for off in range(1, n):
        peer = (me + off) % n
        i = off - 1
        copies.append(remote(s_ref.at[peer], got_s.at[i], send_s.at[i], recv_s.at[i], seq=peer))
        copies.append(remote(o_ref.at[peer], got_o.at[i], send_o.at[i], recv_o.at[i], seq=peer))
    for copy in copies:
        copy.start()

    tall, wide = share * SUF_ROWS, SUF_ROWS * span
    at = lax.broadcasted_iota(jnp.int32, (tall, wide), 1)
    own_row = lax.broadcasted_iota(jnp.int32, (tall, wide), 0) % SUF_ROWS
    offset = at - own_row * span

    def suffix(b, carry):
        block = pl.ds(pl.multiple_of(b * SUF_ROWS, SUF_ROWS), SUF_ROWS)
        lens = jnp.concatenate([len_ref[block, :]] * share, axis=0)
        live = (offset >= 0) & (offset < lens)
        found = []
        for h in range(kv_local):
            q = jnp.concatenate(
                [q_ref[block, (h * share + g) * HD:(h * share + g + 1) * HD] for g in range(share)],
                axis=0,
            )
            k = k_ref[block, :, h * HD:(h + 1) * HD].reshape(wide, HD)
            v = v_ref[block, :, h * HD:(h + 1) * HD].reshape(wide, HD)
            s = lax.dot_general(
                q, k, (((1,), (1,)), ((), ())), preferred_element_type=F32
            ) * scale
            s = jnp.where(live, s, NEG)
            m = jnp.max(s, axis=1, keepdims=True)
            w = jnp.exp(s - m)
            total = jnp.sum(w, axis=1, keepdims=True)
            o = jnp.dot(w.astype(BF16), v, preferred_element_type=F32) / total
            lse = m + jnp.log(total)
            for g in range(share):
                part = slice(g * SUF_ROWS, (g + 1) * SUF_ROWS)
                suf_o[block, (h * share + g) * HD:(h * share + g + 1) * HD] = o[part]
                found.append(lse[part])
        if heads < HD:
            found.append(jnp.zeros((SUF_ROWS, HD - heads), F32))
        suf_s[block, :] = jnp.concatenate(found, axis=1)
        return carry

    lax.fori_loop(0, rows // SUF_ROWS, suffix, 0)
    for copy in copies:
        copy.wait()

    stats = [suf_s[...], s_ref[me]] + [got_s[i] for i in range(n - 1)]
    best = functools.reduce(jnp.maximum, stats)
    weights = [jnp.exp(one - best) for one in stats]
    total = functools.reduce(jnp.add, weights)
    weights = [one / total for one in weights]
    for h in range(heads):
        cols = slice(h * HD, (h + 1) * HD)
        mixed = weights[0][:, h:h + 1] * suf_o[:, cols]
        mixed = mixed + weights[1][:, h:h + 1] * o_ref[me, :, cols].astype(F32)
        for i in range(n - 1):
            mixed = mixed + weights[2 + i][:, h:h + 1] * got_o[i, :, cols].astype(F32)
        out_ref[:, cols] = mixed.astype(BF16)


def project_kernel(n, reps, tps, att_ref, w_ref, out_ref, every, parts, got, own,
                   send_r, recv_r, send_l, recv_l, send_x, recv_x, send_t, recv_t, own_sem):
    me, rep, tp = lax.axis_index("seq"), lax.axis_index("rep"), lax.axis_index("tp")
    distances = []
    d = reps // 2
    while d >= 1:
        distances.append(d)
        d //= 2

    def across(r, d):
        return r + d - 2 * d * ((r // d) % 2)

    if n > 1:
        greet_line(me, n)
    for d in distances:
        signal(rep=across(rep, d))
    for off in range(1, tps):
        signal(tp=(tp + off) % tps)
    local = pltpu.make_async_copy(att_ref, every.at[rep * n + me], own_sem)
    local.start()
    local.wait()
    await_greetings(me, n, len(distances) + tps - 1)

    def right(j):
        place = every.at[rep * n + j]
        return remote(place, place, send_r.at[j], recv_r.at[j], seq=me + 1)

    def left(j):
        place = every.at[rep * n + j]
        return remote(place, place, send_l.at[j], recv_l.at[j], seq=me - 1)

    def over(stage, r, j):
        place = every.at[r * n + j]
        return remote(place, place, send_x.at[stage, r * n + j], recv_x.at[r * n + j],
                      rep=across(rep, distances[stage]))

    def hop(t, carry):
        j = me - t

        @pl.when(j >= 0)
        def _():
            @pl.when(t > 0)
            def _():
                right(j).wait_recv()

            @pl.when(me < n - 1)
            def _():
                right(j).start()

            for stage in range(len(distances)):
                over(stage, rep, j).start()

        e = me + t

        @pl.when(e < n)
        def _():
            @pl.when(t > 0)
            def _():
                left(e).wait_recv()
                for stage in range(len(distances)):
                    over(stage, rep, e).start()

            @pl.when(me > 0)
            def _():
                left(e).start()

        return carry

    lax.fori_loop(0, n, hop, 0)

    held = [rep]
    for stage in range(len(distances)):
        arrived = [across(r, distances[stage]) for r in held]
        for r in arrived:
            def pass_on(j, carry, r=r, stage=stage):
                over(stage, r, j).wait_recv()
                for later in range(stage + 1, len(distances)):
                    over(later, r, j).start()
                return carry

            lax.fori_loop(0, n, pass_on, 0)
        held = held + arrived

    blocks, tall = every.shape[0], every.shape[1]
    share = blocks // tps
    unit = min(share, max(1, 256 // tall))

    def rows_of(peer, put):
        def piece(u, carry):
            x = every[pl.ds(peer * share + u * unit, unit)].reshape(unit * tall, -1)
            y = jnp.dot(x, w_ref[...], preferred_element_type=F32)
            put(u, pl.ds(pl.multiple_of(u * unit * tall, unit * tall), unit * tall), y)
            return carry

        lax.fori_loop(0, share // unit, piece, 0)

    def swap(i, peer, u):
        where = pl.ds(pl.multiple_of(u * unit * tall, unit * tall), unit * tall)
        return remote(parts.at[i, where], got.at[i, where], send_t.at[i, u], recv_t.at[i, u],
                      tp=peer)

    for off in range(1, tps):
        peer = (tp + off) % tps
        i = off - 1

        def put(u, where, y, i=i, peer=peer):
            parts[i, where, :] = y.astype(BF16)
            swap(i, peer, u).start()

        rows_of(peer, put)

    def put_own(u, where, y):
        own[where, :] = y

    rows_of(tp, put_own)
    for off in range(1, tps):
        for u in range(share // unit):
            swap(off - 1, (tp + off) % tps, u).wait()
    result = own[...]
    for i in range(tps - 1):
        result = result + got[i].astype(F32)
    out_ref[...] = result.astype(BF16)

    def drain(j, carry):
        @pl.when((j <= me) & (me < n - 1))
        def _():
            right(j).wait_send()

        @pl.when((j >= me) & (me > 0))
        def _():
            left(j).wait_send()

        return carry

    lax.fori_loop(0, n, drain, 0)
    held = [rep]
    for stage in range(len(distances)):
        for r in held:
            def sent(j, carry, r=r, stage=stage):
                over(stage, r, j).wait_send()
                return carry

            lax.fori_loop(0, n, sent, 0)
        held = held + [across(r, distances[stage]) for r in held]


def params(number):
    return pltpu.CompilerParams(
        collective_id=number, has_side_effects=True, vmem_limit_bytes=VMEM_LIMIT
    )


def vmem():
    return pl.BlockSpec(memory_space=pltpu.VMEM)


def body(
    counts,
    prompt_of,
    queries,
    new_kv,
    prompt_keys,
    prompt_values,
    suffix_keys,
    suffix_values,
    gen_len,
    out_weight,
):
    n = lax.axis_size("seq")
    reps = lax.axis_size("rep")
    tps = lax.axis_size("tp")
    me = lax.axis_index("seq")
    capacity, width = queries.shape[1:]
    kv_width = new_kv.shape[3]
    kv_local = kv_width // HD
    heads = width // HD
    share = heads // kv_local
    per_device = gen_len.shape[1]
    group_rows = per_device * n
    prompts, positions = prompt_keys.shape[1:3]
    block_rows = group_rows // prompts
    chunks = width // CHUNK

    tally = counts[0]
    start = jnp.sum(jnp.where(jnp.arange(n, dtype=jnp.int32) < me, tally, 0))
    count = jnp.sum(jnp.where(jnp.arange(n, dtype=jnp.int32) == me, tally, 0))
    row_ids = jnp.arange(group_rows, dtype=jnp.int32)
    of = prompt_of[0]
    before = (of[None, :] < of[:, None]) | (
        (of[None, :] == of[:, None]) & (row_ids[None, :] < row_ids[:, None])
    )
    rank = jnp.sum(before.astype(jnp.int32), axis=1)
    place = (rank[None, :] == row_ids[:, None]).astype(BF16)
    back = (rank[:, None] == row_ids[None, :]).astype(BF16)
    row_of = jnp.sum(jnp.where(rank[None, :] == row_ids[:, None], row_ids[None, :], 0), axis=1)
    slot = row_of - start
    mine = (slot >= 0) & (slot < count)
    picker = (
        (slot[:, None] == jnp.arange(capacity, dtype=jnp.int32)[None, :]) & mine[:, None]
    ).astype(BF16)
    fresh = jnp.dot(
        picker, new_kv[0].reshape(capacity, 2 * kv_width), preferred_element_type=F32
    ).astype(BF16)
    held = mine.astype(F32)[:, None]

    chunk_shape = (chunks, group_rows, CHUNK)
    sorted_q = pl.pallas_call(
        functools.partial(spread_kernel, n),
        out_shape=jax.ShapeDtypeStruct(chunk_shape, BF16),
        in_specs=[vmem(), vmem()],
        out_specs=vmem(),
        scratch_shapes=[pltpu.VMEM(chunk_shape, BF16)] * 5
        + [pltpu.SemaphoreType.DMA((chunks,))] * 4,
        compiler_params=params(0),
        name="spread_queries",
    )(picker, queries[0])

    per = share * HD // CHUNK
    at_once = PROMPTS_STEP if prompts % PROMPTS_STEP == 0 else 1
    step_rows = at_once * block_rows
    partial_o, lse = pl.pallas_call(
        functools.partial(prompt_kernel, share),
        grid=(kv_local, prompts // at_once),
        out_shape=(
            jax.ShapeDtypeStruct((group_rows, width), BF16),
            jax.ShapeDtypeStruct((kv_local, group_rows, share), F32),
        ),
        in_specs=[
            pl.BlockSpec((per, step_rows, CHUNK), lambda h, p: (h, p, 0)),
            pl.BlockSpec((at_once, positions, HD), lambda h, p: (p, 0, h)),
            pl.BlockSpec((at_once, positions, HD), lambda h, p: (p, 0, h)),
            pl.BlockSpec((step_rows, HD), lambda h, p: (p, h)),
            pl.BlockSpec((step_rows, HD), lambda h, p: (p, h + kv_local)),
            pl.BlockSpec((step_rows, 1), lambda h, p: (p, 0)),
        ],
        out_specs=(
            pl.BlockSpec((step_rows, share * HD), lambda h, p: (p, h)),
            pl.BlockSpec((1, step_rows, share), lambda h, p: (h, p, 0)),
        ),
        compiler_params=pltpu.CompilerParams(vmem_limit_bytes=VMEM_LIMIT),
        name="prompt_attention",
    )(sorted_q, prompt_keys[0], prompt_values[0], fresh, fresh, held)

    row_o = jnp.dot(back, partial_o, preferred_element_type=F32).astype(BF16)
    row_s = jnp.take(jnp.swapaxes(lse, 0, 1).reshape(group_rows, heads), rank, axis=0)
    row_s = jnp.pad(row_s, ((0, 0), (0, HD - heads)))
    own_back = lax.dynamic_slice_in_dim(back, me * per_device, per_device, 0)
    own_q = jnp.einsum("rp,cpw->rcw", own_back, sorted_q, preferred_element_type=F32)
    own_q = own_q.astype(BF16).reshape(per_device, width)

    attended = pl.pallas_call(
        functools.partial(combine_kernel, n, kv_local, share),
        out_shape=jax.ShapeDtypeStruct((per_device, width), BF16),
        in_specs=[vmem()] * 6,
        out_specs=vmem(),
        scratch_shapes=[
            pltpu.VMEM((max(1, n - 1), per_device, width), BF16),
            pltpu.VMEM((max(1, n - 1), per_device, HD), F32),
            pltpu.VMEM((per_device, width), F32),
            pltpu.VMEM((per_device, HD), F32),
        ]
        + [pltpu.SemaphoreType.DMA((max(1, n - 1),))] * 4,
        compiler_params=params(1),
        name="exchange_and_suffix",
    )(
        row_o.reshape(n, per_device, width),
        row_s.reshape(n, per_device, HD),
        own_q,
        suffix_keys[0],
        suffix_values[0],
        gen_len[0][:, None],
    )

    columns = out_weight.shape[1]
    out_rows = group_rows * reps // tps
    stages = max(1, reps.bit_length() - 1)
    dma = pltpu.SemaphoreType.DMA
    return pl.pallas_call(
        functools.partial(project_kernel, n, reps, tps),
        out_shape=jax.ShapeDtypeStruct((out_rows, columns), BF16),
        in_specs=[vmem()] * 2,
        out_specs=vmem(),
        scratch_shapes=[
            pltpu.VMEM((reps * n, per_device, width), BF16),
            pltpu.VMEM((max(1, tps - 1), out_rows, columns), BF16),
            pltpu.VMEM((max(1, tps - 1), out_rows, columns), BF16),
            pltpu.VMEM((out_rows, columns), F32),
            dma((n,)), dma((n,)), dma((n,)), dma((n,)),
            dma((stages, reps * n)), dma((reps * n,)),
            dma((max(1, tps - 1), reps * n)), dma((max(1, tps - 1), reps * n)),
            pltpu.SemaphoreType.DMA,
        ],
        compiler_params=params(2),
        name="gather_and_project",
    )(attended, out_weight)


def solution(mesh):
    in_specs = (
        P("rep", None),
        P("rep", None),
        P("rep", "seq", "tp"),
        P("rep", "seq", None, "tp"),
        P("rep", None, "seq", "tp"),
        P("rep", None, "seq", "tp"),
        P("rep", "seq", None, "tp"),
        P("rep", "seq", None, "tp"),
        P("rep", "seq"),
        P("tp", ("seq", "rep")),
    )
    out_specs = P("tp", ("seq", "rep"))
    return jax.shard_map(body, mesh=mesh, in_specs=in_specs, out_specs=out_specs, check_vma=False)
```
